32 devices in a mesh: dp: 16 (over z, y, core), tensor: 2 (over x).
Axes of the slice: x: 2, y: 2, z: 4, core: 2. Of those that a mesh axis runs over, the one named last changes fastest.
Arguments:
- queries: bfloat16 [32, 256, 8192], P('dp', None, 'tensor'), may hold values from -5 to 5
- resp_kv: bfloat16 [32, 256, 2, 1024], P('dp', None, None, 'tensor'), may hold values from -12 to 12
- prefix_pool: bfloat16 [512, 2, 2, 1024], P(('dp', 'tensor')), may hold values from -12 to 12
- grad_out: bfloat16 [32, 256, 8192], P('dp', None, 'tensor'), may hold values from -12 to 12
- member_list: int32 [2, 8], replicated, may hold values from 0 to 15, as said below
- prompt_slot: int32 [2], replicated, may hold values from 0 to 1, each once
- resp_len: int32 [32], P('dp'), may hold values from 1 to 256, 5120 in all
Outputs:
- attention: bfloat16 [32, 256, 8192], P('dp', None, 'tensor')
- grad_queries: bfloat16 [32, 256, 8192], P('dp', None, 'tensor')
- grad_resp_kv: bfloat16 [32, 256, 2, 1024], P('dp', None, None, 'tensor')
- grad_prefix: bfloat16 [512, 2, 2, 1024], P(('dp', 'tensor'))
The draws below stay inside these ranges and needn't reach their ends.
Inputs may be any that keep to these rules, and one draw needn't show every extreme that they name: `member_list`: each dp index appears exactly once.
All inputs are finite; a program needn't handle non-finite values. No bound on the sum of `resp_len` on one device may be relied on, other than what follows from the above.
Results may differ from the reference program's by a relative error of at most 0.024.
Values may be sent and summed in bfloat16 or wider, within the bound.
No kernel may reach another device: no remote copies, remote signals or barrier semaphores. Data moves between devices by JAX's collectives and lax.ppermute only.
A program may use at most 128 MiB of HBM per device.

```python
import math
import jax
import jax.numpy as jnp
import numpy as np
from jax import lax

QUERY_HEADS = 64
KEY_VALUE_HEADS = 8
HEAD_SIZE = 128
RESP_DEV = 2
RESPONSE_LENGTH = 256
PROMPT_LENGTH = 512
GROUP = 8
RESPONSE_TOTAL = 32
PROMPT_TOTAL = 2


def rows_after_scale(key, array_shape, spread_lo, spread_hi):
    return jnp.exp(jax.random.uniform(key, array_shape, minval=jnp.log(spread_lo), maxval=jnp.log(spread_hi)))


def draw_queries(key, part):
    key = jax.random.fold_in(key, 1)
    key_one = jax.random.fold_in(key, 0)
    sample_draw = jnp.clip(jax.random.normal(key_one, (RESPONSE_TOTAL, RESPONSE_LENGTH, QUERY_HEADS, HEAD_SIZE)), -4.0, 4.0)
    return sample_draw.reshape(RESPONSE_TOTAL, RESPONSE_LENGTH, QUERY_HEADS * HEAD_SIZE).astype(jnp.bfloat16)


def draw_resp_kv(key, part):
    key = jax.random.fold_in(key, 2)
    key_one, second_random_key = jax.random.split(key, 2)
    array_shape = (RESPONSE_TOTAL, RESPONSE_LENGTH, 2, KEY_VALUE_HEADS, HEAD_SIZE)
    row_factor_scale = rows_after_scale(second_random_key, (RESPONSE_TOTAL, RESPONSE_LENGTH, 2, KEY_VALUE_HEADS, 1), 0.3, 3.0)
    sample_draw = jnp.clip(jax.random.normal(key_one, array_shape), -4.0, 4.0) * row_factor_scale
    return sample_draw.reshape(RESPONSE_TOTAL, RESPONSE_LENGTH, 2, KEY_VALUE_HEADS * HEAD_SIZE).astype(jnp.bfloat16)


def draw_prefix_pool(key, part):
    key = jax.random.fold_in(key, 3)
    key_one, second_random_key = jax.random.split(key, 2)
    array_shape = (PROMPT_LENGTH, PROMPT_TOTAL, 2, KEY_VALUE_HEADS, HEAD_SIZE)
    row_factor_scale = rows_after_scale(second_random_key, (PROMPT_LENGTH, PROMPT_TOTAL, 2, KEY_VALUE_HEADS, 1), 0.3, 3.0)
    sample_draw = jnp.clip(jax.random.normal(key_one, array_shape), -4.0, 4.0) * row_factor_scale
    return sample_draw.reshape(PROMPT_LENGTH, PROMPT_TOTAL, 2, KEY_VALUE_HEADS * HEAD_SIZE).astype(jnp.bfloat16)


def draw_member_list(key, part):
    key = jax.random.fold_in(key, 4)
    order = jax.random.permutation(key, RESPONSE_TOTAL // RESP_DEV)
    return order.reshape(PROMPT_TOTAL, GROUP).astype(jnp.int32)


def shard_levels(stream_key, extent, pieces, least, high):
    loudness, own = 1.0, jax.random.fold_in(stream_key, 6)
    for dim, parts in pieces:
        draws = jnp.exp(jax.random.uniform(jax.random.fold_in(own, dim), (parts,), jnp.float32, least / len(pieces), high / len(pieces)))
        loudness = loudness * jnp.repeat(draws, extent[dim] // parts).reshape([-1 if axis == dim else 1 for axis in range(len(extent))])
    return loudness


def length_profile(number_of, total, bound, slope):
    weights = [(1 << 20) // math.isqrt(standing ** slope) + 1 for standing in range(2, number_of + 1)]
    rest, counts = total - bound - (number_of - 1), [1] * (number_of - 1)
    while rest > 0:
        free = [i for i in range(number_of - 1) if counts[i] < bound]
        pool, left = sum([weights[i] for i in free]), rest
        for i in free:
            addition = min(bound - counts[i], max(1, left * weights[i] // pool), rest)
            counts[i] = counts[i] + addition
            rest = rest - addition
    return np.array([bound] + counts)


def ragged_sizes(key, count, total, limit, skew):
    if count == 2:
        one = jax.random.randint(key, (), max(1, total - limit), min(limit, total - 1) + 1)
        return jnp.stack([one, total - one])
    sizes = jnp.asarray(length_profile(count, total, limit, skew), jnp.int32)
    twos = (count - 1) // 2
    donor, sink = sizes[1:1 + 2 * twos:2], sizes[2:2 + 2 * twos:2]
    slack = jnp.minimum(donor - 1, limit - sink)
    moved = jax.random.randint(jax.random.fold_in(key, 1), (twos,), 0, 1 << 20) % (slack + 1)
    sizes = sizes.at[1:1 + 2 * twos:2].set(donor - moved).at[2:2 + 2 * twos:2].set(sink + moved)
    return sizes[jax.random.permutation(jax.random.fold_in(key, 2), count)]


def normal_values(own_key, dims, spread, most, pieces=(), held_as=jnp.bfloat16):
    entries = spread * jax.random.normal(own_key, dims, jnp.float32)
    if pieces:
        entries = entries * shard_levels(own_key, dims, pieces, -0.22, 0.18)
    return jnp.clip(entries, -most, most).astype(held_as)


def setup_inputs(seed: int = 0) -> dict:
    key_of = jax.random.split(jax.random.key(seed), 8)
    return {
        "queries": draw_queries(jax.random.fold_in(key_of[7], 71), 0),
        "resp_kv": draw_resp_kv(jax.random.fold_in(key_of[7], 71), 0),
        "prefix_pool": draw_prefix_pool(jax.random.fold_in(key_of[7], 71), 0),
        "grad_out": normal_values(key_of[3], (RESPONSE_TOTAL, RESPONSE_LENGTH, QUERY_HEADS * HEAD_SIZE), 2.0, 12.0, ((0, 16), (2, 2))),
        "member_list": draw_member_list(jax.random.fold_in(key_of[7], 71), 0),
        "prompt_slot": jax.random.permutation(key_of[5], PROMPT_TOTAL).astype(jnp.int32),
        "resp_len": ragged_sizes(key_of[6], RESPONSE_TOTAL, RESPONSE_TOTAL * RESPONSE_LENGTH * 5 // 8, RESPONSE_LENGTH, 1).astype(jnp.int32),
    }


def reference(queries, resp_kv, prefix_pool, grad_out, member_list, prompt_slot, resp_len):
    heads_per_group = QUERY_HEADS // KEY_VALUE_HEADS
    score_scale = HEAD_SIZE ** -0.5
    device_count = RESPONSE_TOTAL // RESP_DEV
    owner_hit = member_list[:, :, None] == jnp.arange(device_count, dtype=jnp.int32)[None, None, :]
    prompt_of = jnp.sum(jnp.where(owner_hit, jnp.arange(PROMPT_TOTAL, dtype=jnp.int32)[:, None, None], 0), axis=(0, 1)).astype(jnp.int32)
    slot_of = prompt_slot[prompt_of]
    position = jnp.arange(RESPONSE_LENGTH, dtype=jnp.int32)
    visible = jnp.concatenate([jnp.ones((RESPONSE_LENGTH, PROMPT_LENGTH), dtype=bool), position[None, :] <= position[:, None]], axis=1)

    def one_response(prefix_grad, response_tokens):
        pool_slot = slot_of[response_tokens // RESP_DEV]
        prefix_rows = lax.dynamic_index_in_dim(prefix_pool, pool_slot, 1, keepdims=False)
        every_key_value = jnp.concatenate([prefix_rows, resp_kv[response_tokens]], axis=0)
        every_key_value = every_key_value.reshape(PROMPT_LENGTH + RESPONSE_LENGTH, 2, KEY_VALUE_HEADS, HEAD_SIZE).astype(jnp.float32)
        key_rows = every_key_value[:, 0]
        value_rows = every_key_value[:, 1]
        query_matrix = queries[response_tokens].reshape(RESPONSE_LENGTH, KEY_VALUE_HEADS, heads_per_group, HEAD_SIZE).astype(jnp.float32)
        scores = jnp.einsum('sgeh,jgh->gesj', query_matrix, key_rows) * score_scale
        scores = jnp.where(visible, scores, -jnp.inf)
        row_peak = jnp.max(scores, axis=-1, keepdims=True)
        exp_scores = jnp.exp(scores - row_peak)
        probs = exp_scores / jnp.sum(exp_scores, axis=-1, keepdims=True)
        probs_b = lax.optimization_barrier(probs.astype(jnp.bfloat16))
        live_rows = (position < resp_len[response_tokens]).astype(jnp.float32)
        attended = jnp.einsum('gesj,jgh->sgeh', probs_b.astype(jnp.float32), value_rows)
        attention = lax.optimization_barrier((attended * live_rows[:, None, None, None]).astype(jnp.bfloat16))
        active_gradient = (grad_out[response_tokens].astype(jnp.float32) * live_rows[:, None]).astype(jnp.bfloat16)
        active_gradient = lax.optimization_barrier(active_gradient).reshape(RESPONSE_LENGTH, KEY_VALUE_HEADS, heads_per_group, HEAD_SIZE).astype(jnp.float32)
        row_delta = jnp.einsum('sgeh,sgeh->ges', active_gradient, attention.astype(jnp.float32))
        dprobs = jnp.einsum('sgeh,jgh->gesj', active_gradient, value_rows)
        dscores = lax.optimization_barrier((probs * (dprobs - row_delta[..., None])).astype(jnp.bfloat16))
        dscores = dscores.astype(jnp.float32)
        grad_query = (jnp.einsum('gesj,jgh->sgeh', dscores, key_rows) * score_scale).astype(jnp.bfloat16)
        key_gradient = jnp.einsum('gesj,sgeh->jgh', dscores, query_matrix) * score_scale
        value_gradient = jnp.einsum('gesj,sgeh->jgh', probs_b.astype(jnp.float32), active_gradient)
        key_value_gradient = jnp.stack([key_gradient, value_gradient], axis=1).reshape(PROMPT_LENGTH + RESPONSE_LENGTH, 2, KEY_VALUE_HEADS * HEAD_SIZE)
        slot_hot = (jnp.arange(PROMPT_TOTAL, dtype=jnp.int32) == pool_slot).astype(jnp.float32)
        prefix_grad = prefix_grad + key_value_gradient[:PROMPT_LENGTH, None] * slot_hot[None, :, None, None]
        outputs = (attention.reshape(RESPONSE_LENGTH, QUERY_HEADS * HEAD_SIZE), grad_query.reshape(RESPONSE_LENGTH, QUERY_HEADS * HEAD_SIZE), key_value_gradient[PROMPT_LENGTH:].astype(jnp.bfloat16))
        return prefix_grad, outputs

    empty_gradient = jnp.zeros((PROMPT_LENGTH, PROMPT_TOTAL, 2, KEY_VALUE_HEADS * HEAD_SIZE), dtype=jnp.float32)
    prefix_grad, stacked = lax.scan(one_response, empty_gradient, jnp.arange(RESPONSE_TOTAL, dtype=jnp.int32))
    return stacked[0], stacked[1], stacked[2], prefix_grad.astype(jnp.bfloat16)
```

```python
import functools
import math

import jax
import jax.numpy as jnp
from jax import lax
from jax.experimental import pallas as pl
from jax.experimental.pallas import tpu as pltpu
from jax.sharding import PartitionSpec as P

HEAD = 128
F32 = jnp.float32
BF16 = jnp.bfloat16
SCALE = HEAD ** (-0.5)
LOG2_SCALE = SCALE * math.log2(math.e)
NT = ((1,), (1,))
NN = ((1,), (0,))
TN = ((0,), (0,))


def dot(a, b, dims):
    return lax.dot_general(a, b, (dims, ((), ())), preferred_element_type=F32)


def attention_kernel(
    tile_rows,
    head_block,
    group,
    len_ref,
    query_ref,
    grad_ref,
    far_key_ref,
    far_value_ref,
    own_key_ref,
    own_value_ref,
    out_ref,
    dquery_ref,
    own_dkey_ref,
    own_dvalue_ref,
    far_dkey_ref,
    far_dvalue_ref,
    far_dk,
    far_dv,
    own_dk,
    own_dv,
):
    response = pl.program_id(1)
    live_count = len_ref[response]
    row_count = query_ref.shape[1]
    tall = head_block * tile_rows

    @pl.when(response == 0)
    def _():
        far_dk[...] = jnp.zeros_like(far_dk)
        far_dv[...] = jnp.zeros_like(far_dv)

    own_dk[...] = jnp.zeros_like(own_dk)
    own_dv[...] = jnp.zeros_like(own_dv)

    def tile(first_row, first_head):
        columns = [
            pl.ds(pl.multiple_of((first_head + j) * HEAD, HEAD), HEAD) for j in range(head_block)
        ]
        rows = pl.ds(first_row, tile_rows)
        near_count = first_row + tile_rows
        query = jnp.concatenate([query_ref[0, rows, c] for c in columns], 0)
        grad = jnp.concatenate([grad_ref[0, rows, c] for c in columns], 0)
        far_key = far_key_ref[...]
        far_value = far_value_ref[...]
        own_key = own_key_ref[0, pl.ds(0, near_count), :]
        own_value = own_value_ref[0, pl.ds(0, near_count), :]
        row_in_tile = lax.broadcasted_iota(jnp.int32, (tall, 1), 0) % tile_rows
        live = row_in_tile + first_row < live_count
        far_score = dot(query, far_key, NT)
        near_score = dot(query, own_key, NT)
        row = lax.broadcasted_iota(jnp.int32, (tall, tile_rows), 0) % tile_rows
        column = lax.broadcasted_iota(jnp.int32, (tall, tile_rows), 1)
        corner = jnp.where(column <= row, near_score[:, first_row:], -jnp.inf)
        near_score = jnp.concatenate([near_score[:, :first_row], corner], 1) if first_row else corner
        peak = jnp.maximum(
            jnp.max(far_score, 1, keepdims=True), jnp.max(near_score, 1, keepdims=True)
        )
        far_exp = jnp.exp2((far_score - peak) * LOG2_SCALE)
        near_exp = jnp.exp2((near_score - peak) * LOG2_SCALE)
        total = jnp.sum(far_exp, 1, keepdims=True) + jnp.sum(near_exp, 1, keepdims=True)
        inverse = jnp.where(live, 1.0 / total, 0.0)
        far_b = far_exp.astype(BF16)
        near_b = near_exp.astype(BF16)
        out = ((dot(far_b, far_value, NN) + dot(near_b, own_value, NN)) * inverse).astype(BF16)
        grad = (grad.astype(F32) * inverse).astype(BF16)
        delta = jnp.sum(grad.astype(F32) * out.astype(F32), 1, keepdims=True)
        far_ds = (far_exp * (dot(grad, far_value, NT) - delta)).astype(BF16)
        near_ds = (near_exp * (dot(grad, own_value, NT) - delta)).astype(BF16)
        dquery = ((dot(far_ds, far_key, NN) + dot(near_ds, own_key, NN)) * SCALE).astype(BF16)
        for j, c in enumerate(columns):
            out_ref[0, rows, c] = out[j * tile_rows : (j + 1) * tile_rows]
            dquery_ref[0, rows, c] = dquery[j * tile_rows : (j + 1) * tile_rows]
        far_dk[...] += dot(query, far_ds, TN)
        far_dv[...] += dot(grad, far_b, TN)
        own_dk[:, :near_count] += dot(query, near_ds, TN)
        own_dv[:, :near_count] += dot(grad, near_b, TN)

    for first_row in range(0, row_count, tile_rows):

        @pl.when(first_row < live_count)
        def _(first_row=first_row):
            def step(i, carry):
                tile(first_row, i * head_block)
                return carry

            lax.fori_loop(0, group // head_block, step, 0)

        if first_row:

            @pl.when(first_row >= live_count)
            def _(first_row=first_row):
                blank = jnp.zeros((tile_rows, group * HEAD), BF16)
                out_ref[0, pl.ds(first_row, tile_rows), :] = blank
                dquery_ref[0, pl.ds(first_row, tile_rows), :] = blank

    own_dkey_ref[0] = (own_dk[...].T * SCALE).astype(BF16)
    own_dvalue_ref[0] = own_dv[...].T.astype(BF16)

    @pl.when(response == pl.num_programs(1) - 1)
    def _():
        far_dkey_ref[...] = (far_dk[...].T * SCALE).astype(BF16)
        far_dvalue_ref[...] = far_dv[...].T.astype(BF16)


def attention_grads(queries, grad_out, own_kv, prefix, resp_len):
    responses, rows, width = queries.shape
    kv_local = own_kv.shape[2] // (2 * HEAD)
    group = width // HEAD // kv_local
    prompt_rows = prefix.shape[0]
    tile_rows = 128
    head_block = math.gcd(group, 4)
    wide = pl.BlockSpec((1, rows, group * HEAD), lambda a, r, *_: (r, 0, a))
    own_k = pl.BlockSpec((1, rows, HEAD), lambda a, r, *_: (r, 0, a))
    own_v = pl.BlockSpec((1, rows, HEAD), lambda a, r, *_: (r, 0, kv_local + a))
    far_k = pl.BlockSpec((prompt_rows, HEAD), lambda a, r, *_: (0, a))
    far_v = pl.BlockSpec((prompt_rows, HEAD), lambda a, r, *_: (0, kv_local + a))
    own_shape = jax.ShapeDtypeStruct((responses, rows, kv_local * HEAD), BF16)
    far_shape = jax.ShapeDtypeStruct((prompt_rows, kv_local * HEAD), BF16)
    return pl.pallas_call(
        functools.partial(attention_kernel, tile_rows, head_block, group),
        grid_spec=pltpu.PrefetchScalarGridSpec(
            num_scalar_prefetch=1,
            grid=(kv_local, responses),
            in_specs=[wide, wide, far_k, far_v, own_k, own_v],
            out_specs=[wide, wide, own_k, own_k, far_k, far_k],
            scratch_shapes=[
                pltpu.VMEM((HEAD, prompt_rows), F32),
                pltpu.VMEM((HEAD, prompt_rows), F32),
                pltpu.VMEM((HEAD, rows), F32),
                pltpu.VMEM((HEAD, rows), F32),
            ],
        ),
        out_shape=[
            jax.ShapeDtypeStruct(queries.shape, BF16),
            jax.ShapeDtypeStruct(queries.shape, BF16),
            own_shape,
            own_shape,
            far_shape,
            far_shape,
        ],
        compiler_params=pltpu.CompilerParams(vmem_limit_bytes=48 << 20),
        name="attention_grads",
    )(resp_len, queries, grad_out, prefix, prefix, own_kv, own_kv)


def on_device(queries, resp_kv, prefix_pool, grad_out, member_list, prompt_slot, resp_len):
    dp_count = lax.axis_size("dp")
    tensor_count = lax.axis_size("tensor")
    responses, rows = queries.shape[:2]
    kv_width = resp_kv.shape[3]
    slice_rows, slot_count = prefix_pool.shape[:2]
    prompt_count = member_list.shape[0]
    everyone = ("dp", "tensor")

    owner_hit = member_list[:, :, None] == jnp.arange(dp_count, dtype=jnp.int32)[None, None, :]
    slot_of = jnp.sum(jnp.where(owner_hit, prompt_slot[:, None, None], 0), axis=(0, 1))

    pool = prefix_pool.reshape(slice_rows, slot_count, 2, tensor_count, kv_width)
    wanted = slot_of[:, None, None, None, None]
    outgoing = jnp.zeros((), BF16)
    for slot in range(slot_count):
        part = pool[:, slot].transpose(2, 0, 1, 3)[None]
        outgoing = part if slot == 0 else jnp.where(wanted == slot, part, outgoing)
    outgoing = outgoing.reshape(dp_count * tensor_count, slice_rows, 2 * kv_width)
    prefix = lax.all_to_all(outgoing, everyone, split_axis=0, concat_axis=0, tiled=True)
    prefix = prefix.reshape(dp_count * tensor_count * slice_rows, 2 * kv_width)

    own_kv = resp_kv.reshape(responses, rows, 2 * kv_width)
    attention, grad_queries, own_dk, own_dv, far_dk, far_dv = attention_grads(
        queries, grad_out, own_kv, prefix, resp_len
    )
    grad_resp_kv = jnp.stack([own_dk, own_dv], axis=2)

    partial = jnp.stack([far_dk, far_dv], axis=1)
    partial = partial.reshape(dp_count * tensor_count, slice_rows, 2 * kv_width)
    arrived = lax.all_to_all(partial, everyone, split_axis=0, concat_axis=0, tiled=True)
    arrived = arrived.reshape(dp_count, tensor_count, slice_rows, 2, kv_width).astype(F32)
    sums = []
    for slot in range(slot_count):
        sums.append(jnp.sum(jnp.where(wanted == slot, arrived, 0.0), axis=0))
    grad_prefix = jnp.stack(sums, 0).transpose(2, 0, 3, 1, 4).astype(BF16)
    grad_prefix = grad_prefix.reshape(slice_rows, slot_count, 2, tensor_count * kv_width)
    return attention, grad_queries, grad_resp_kv, grad_prefix


def solution(mesh):
    return jax.shard_map(
        on_device,
        mesh=mesh,
        in_specs=(
            P("dp", None, "tensor"),
            P("dp", None, None, "tensor"),
            P(("dp", "tensor"), None, None, None),
            P("dp", None, "tensor"),
            P(),
            P(),
            P("dp"),
        ),
        out_specs=(
            P("dp", None, "tensor"),
            P("dp", None, "tensor"),
            P("dp", None, None, "tensor"),
            P(("dp", "tensor"), None, None, None),
        ),
        check_vma=False,
    )
```

```python
import functools
import math

import jax
import jax.numpy as jnp
from jax import lax
from jax.experimental import pallas as pl
from jax.experimental.pallas import tpu as pltpu
from jax.sharding import PartitionSpec as P

HEAD = 128
F32 = jnp.float32
BF16 = jnp.bfloat16
SCALE = HEAD ** (-0.5)
LOG2_SCALE = SCALE * math.log2(math.e)
NT = ((1,), (1,))
NN = ((1,), (0,))
TN = ((0,), (0,))
EVERYONE = ("dp", "tensor")
VMEM_LIMIT = 56 << 20


def dot(a, b, dims):
    return lax.dot_general(a, b, (dims, ((), ())), preferred_element_type=F32)


def attention_kernel(tile_rows, head_block, group, *refs):
    len_ref, query_ref, grad_ref, far_ref, own_key_ref, own_value_ref = refs[:6]
    out_ref, dquery_ref, own_dkey_ref, own_dvalue_ref, far_grad_ref = refs[-9:-4]
    keys, values, dkeys, dvalues = refs[-4:]
    response = pl.program_id(1)
    live_count = len_ref[response]
    row_count = query_ref.shape[1]
    prompt_rows = far_ref.shape[0]
    tall = head_block * tile_rows
    far_rows = pl.ds(0, prompt_rows)
    own_rows = pl.ds(prompt_rows, row_count)

    def hold(rows, key, value):
        keys[rows, :HEAD] = key
        keys[rows, HEAD:] = key
        values[rows, :] = value

    @pl.when(response == 0)
    def _():
        hold(far_rows, far_ref[:, :HEAD], far_ref[:, HEAD:])
        dkeys[:, :prompt_rows] = jnp.zeros((HEAD, prompt_rows), F32)
        dvalues[:, :prompt_rows] = jnp.zeros((HEAD, prompt_rows), F32)

    hold(own_rows, own_key_ref[0], own_value_ref[0])
    dkeys[:, prompt_rows:] = jnp.zeros((HEAD, row_count), F32)
    dvalues[:, prompt_rows:] = jnp.zeros((HEAD, row_count), F32)

    def score(c):
        c["query"] = jnp.concatenate([query_ref[0, c["rows"], s] for s in c["columns"]], 0)
        scaled = c["query"].astype(F32) * LOG2_SCALE
        high = scaled.astype(BF16)
        low = (scaled - high.astype(F32)).astype(BF16)
        c["score"] = dot(jnp.concatenate([high, low], 1), keys[: c["count"]], NT)

    def softmax(c):
        scores, count = c.pop("score"), c["count"]
        row = lax.broadcasted_iota(jnp.int32, (tall, tile_rows), 0) % tile_rows
        column = lax.broadcasted_iota(jnp.int32, (tall, tile_rows), 1)
        corner = jnp.where(column <= row, scores[:, count - tile_rows :], -jnp.inf)
        scores = jnp.concatenate([scores[:, : count - tile_rows], corner], 1)
        exps = jnp.exp2(scores - jnp.max(scores, 1, keepdims=True))
        c["exps"] = exps.astype(BF16)
        place = lax.broadcasted_iota(jnp.int32, (tall, 1), 0) % tile_rows + c["first_row"]
        c["inverse"] = jnp.where(
            place < live_count, 1.0 / jnp.sum(exps, 1, keepdims=True), 0.0
        )

    def attend(c):
        inverse, value = c.pop("inverse"), values[: c["count"]]
        out = (dot(c["exps"], value, NN) * inverse).astype(BF16)
        grad = jnp.concatenate([grad_ref[0, c["rows"], s] for s in c["columns"]], 0)
        c["grad"] = grad = (grad.astype(F32) * inverse).astype(BF16)
        c["delta"] = jnp.sum(grad.astype(F32) * out.astype(F32), 1, keepdims=True)
        for j, s in enumerate(c["columns"]):
            out_ref[0, c["rows"], s] = out[j * tile_rows : (j + 1) * tile_rows]
        c["dprobs"] = dot(grad, value, NT)

    def dscore(c):
        c["dscore"] = c["exps"] * (c.pop("dprobs") - c.pop("delta")).astype(BF16)

    def dquery(c):
        result = (dot(c["dscore"], keys[: c["count"], :HEAD], NN) * SCALE).astype(BF16)
        for j, s in enumerate(c["columns"]):
            dquery_ref[0, c["rows"], s] = result[j * tile_rows : (j + 1) * tile_rows]

    def dkey_dvalue(c):
        dkeys[:, : c["count"]] += dot(c["query"], c["dscore"], TN)
        dvalues[:, : c["count"]] += dot(c["grad"], c["exps"], TN)

    stages = (score, softmax, attend, dscore, dquery, dkey_dvalue)

    def work(tiles):
        chains = [
            {
                "columns": [pl.ds((h + j) * HEAD, HEAD) for j in range(head_block)],
                "rows": pl.ds(t, tile_rows),
                "first_row": t,
                "count": prompt_rows + t + tile_rows,
            }
            for h in range(0, group, head_block)
            for t in tiles
        ]
        for step in range(len(stages) + len(chains) - 1):
            for i, chain in enumerate(chains):
                if 0 <= step - i < len(stages):
                    stages[step - i](chain)

    starts = list(range(0, row_count, tile_rows))
    for k in range(len(starts)):
        last = k + 1 == len(starts)
        upper = row_count if last else starts[k + 1]

        @pl.when((live_count > starts[k]) & (last | (live_count <= upper)))
        def _(k=k, last=last, upper=upper):
            work(starts[: k + 1])
            if not last:
                blank = jnp.zeros((row_count - upper, group * HEAD), BF16)
                out_ref[0, upper:, :] = blank
                dquery_ref[0, upper:, :] = blank

    own_dkey_ref[0] = (dkeys[:, prompt_rows:].T * SCALE).astype(BF16)
    own_dvalue_ref[0] = dvalues[:, prompt_rows:].T.astype(BF16)

    @pl.when(response == pl.num_programs(1) - 1)
    def _():
        far_grad_ref[:, :HEAD] = (dkeys[:, :prompt_rows].T * SCALE).astype(BF16)
        far_grad_ref[:, HEAD:] = dvalues[:, :prompt_rows].T.astype(BF16)


def attention_grads(queries, grad_out, own_kv, prefix, resp_len, base, held):
    responses, rows, width = queries.shape
    kv_local = own_kv.shape[2] // (2 * HEAD)
    group = width // HEAD // kv_local
    prompt_rows = prefix.shape[0]
    heads = prefix.shape[1] // (2 * HEAD)
    tile_rows = min(128, rows)
    head_block = math.gcd(group, 4)
    wide = pl.BlockSpec((1, rows, group * HEAD), lambda a, r, *_: (r, 0, a + base))
    own_k = pl.BlockSpec((1, rows, HEAD), lambda a, r, *_: (r, 0, a + base))
    own_v = pl.BlockSpec((1, rows, HEAD), lambda a, r, *_: (r, 0, a + base + kv_local))
    far = pl.BlockSpec((prompt_rows, 2 * HEAD), lambda a, r, *_: (0, a))
    anywhere = pl.BlockSpec(memory_space=pl.ANY)
    own_shape = jax.ShapeDtypeStruct((responses, rows, kv_local * HEAD), BF16)
    pairs = responses * rows * group * heads * (prompt_rows + rows)
    return pl.pallas_call(
        functools.partial(attention_kernel, tile_rows, head_block, group),
        grid_spec=pltpu.PrefetchScalarGridSpec(
            num_scalar_prefetch=1,
            grid=(heads, responses),
            in_specs=[wide, wide, far, own_k, own_v] + [anywhere] * len(held),
            out_specs=[wide, wide, own_k, own_k, far],
            scratch_shapes=[
                pltpu.VMEM((prompt_rows + rows, 2 * HEAD), BF16),
                pltpu.VMEM((prompt_rows + rows, HEAD), BF16),
                pltpu.VMEM((HEAD, prompt_rows + rows), F32),
                pltpu.VMEM((HEAD, prompt_rows + rows), F32),
            ],
        ),
        out_shape=[
            jax.ShapeDtypeStruct(queries.shape, BF16),
            jax.ShapeDtypeStruct(queries.shape, BF16),
            own_shape,
            own_shape,
            jax.ShapeDtypeStruct(prefix.shape, BF16),
        ],
        input_output_aliases={6 + i: i for i in range(len(held))},
        compiler_params=pltpu.CompilerParams(vmem_limit_bytes=VMEM_LIMIT),
        cost_estimate=pl.CostEstimate(
            flops=12 * HEAD * pairs,
            transcendentals=pairs,
            bytes_accessed=8 * responses * rows * group * heads * HEAD,
        ),
        name="attention_grads",
    )(resp_len, queries, grad_out, prefix, own_kv, own_kv, *held)


def outgoing_kernel(shape, chunks, member_ref, slot_ref, pool_ref, *out_refs):
    tensor_count, kv_local = shape
    prompts, members = member_ref.shape
    kv_width = kv_local * HEAD
    half = tensor_count * kv_width

    def one(i, carry):
        prompt = i // members
        owner = member_ref[prompt, i % members]
        start = pl.multiple_of(slot_ref[prompt] * 2 * half, HEAD)
        for t in range(tensor_count):
            for (base, heads), out_ref in zip(chunks, out_refs):
                for h in range(heads):
                    for part in range(2):
                        source = part * half + t * kv_width + (base + h) * HEAD
                        out_ref[owner * tensor_count + t, :, pl.ds((2 * h + part) * HEAD, HEAD)] = (
                            pool_ref[:, pl.ds(pl.multiple_of(start + source, HEAD), HEAD)]
                        )
        return carry

    lax.fori_loop(0, prompts * members, one, 0)


def total_kernel(shape, chunks, member_ref, slot_ref, *refs):
    tensor_count, kv_local = shape
    in_refs, out_ref = refs[:-1], refs[-1]
    prompts, members = member_ref.shape
    kv_width = kv_local * HEAD
    half = tensor_count * kv_width

    def one(prompt, carry):
        start = pl.multiple_of(slot_ref[prompt] * 2 * half, HEAD)
        for (base, heads), in_ref in zip(chunks, in_refs):
            for t in range(tensor_count):
                total = in_ref[member_ref[prompt, 0] * tensor_count + t].astype(F32)
                for m in range(1, members):
                    total += in_ref[member_ref[prompt, m] * tensor_count + t].astype(F32)
                total = total.astype(BF16)
                for h in range(heads):
                    for part in range(2):
                        target = part * half + t * kv_width + (base + h) * HEAD
                        out_ref[:, pl.ds(pl.multiple_of(start + target, HEAD), HEAD)] = total[
                            :, (2 * h + part) * HEAD : (2 * h + part + 1) * HEAD
                        ]
        return carry

    lax.fori_loop(0, prompts, one, 0)


SMEM = pl.BlockSpec(memory_space=pltpu.SMEM)
VMEM = pl.BlockSpec(memory_space=pltpu.VMEM)


def on_device(queries, resp_kv, prefix_pool, grad_out, member_list, prompt_slot, resp_len):
    dp_count = lax.axis_size("dp")
    tensor_count = lax.axis_size("tensor")
    devices = dp_count * tensor_count
    responses, rows = queries.shape[:2]
    kv_width = resp_kv.shape[3]
    kv_local = kv_width // HEAD
    slice_rows, slot_count = prefix_pool.shape[:2]
    shape = (tensor_count, kv_local)
    first = (kv_local + 1) // 2
    chunks = [(0, first)] + ([(first, kv_local - first)] if first < kv_local else [])
    params = pltpu.CompilerParams(vmem_limit_bytes=VMEM_LIMIT)

    outgoing = pl.pallas_call(
        functools.partial(outgoing_kernel, shape, chunks),
        in_specs=[SMEM, SMEM, VMEM],
        out_specs=[VMEM] * len(chunks),
        out_shape=[
            jax.ShapeDtypeStruct((devices, slice_rows, 2 * HEAD * heads), BF16)
            for _, heads in chunks
        ],
        compiler_params=params,
        name="outgoing_rows",
    )(member_list, prompt_slot, prefix_pool.reshape(slice_rows, -1))
    prefixes = [
        lax.all_to_all(block, EVERYONE, split_axis=0, concat_axis=0, tiled=True)
        for block in outgoing
    ]

    own_kv = resp_kv.reshape(responses, rows, 2 * kv_width)
    held, arrived = [], []
    for (base, heads), prefix in zip(chunks, prefixes):
        prefix = prefix.reshape(devices * slice_rows, 2 * HEAD * heads)
        *held, far_grad = attention_grads(
            queries, grad_out, own_kv, prefix, resp_len, base, held
        )
        far_grad = far_grad.reshape(devices, slice_rows, 2 * HEAD * heads)
        arrived.append(
            lax.all_to_all(far_grad, EVERYONE, split_axis=0, concat_axis=0, tiled=True)
        )
    attention, grad_queries, own_dkey, own_dvalue = held
    grad_resp_kv = jnp.stack([own_dkey, own_dvalue], axis=2)

    grad_prefix = pl.pallas_call(
        functools.partial(total_kernel, shape, chunks),
        in_specs=[SMEM, SMEM] + [VMEM] * len(chunks),
        out_specs=VMEM,
        out_shape=jax.ShapeDtypeStruct((slice_rows, prefix_pool.size // slice_rows), BF16),
        compiler_params=params,
        name="prefix_totals",
    )(member_list, prompt_slot, *arrived)
    return attention, grad_queries, grad_resp_kv, grad_prefix.reshape(prefix_pool.shape)


def solution(mesh):
    return jax.shard_map(
        on_device,
        mesh=mesh,
        in_specs=(
            P("dp", None, "tensor"),
            P("dp", None, None, "tensor"),
            P(("dp", "tensor"), None, None, None),
            P("dp", None, "tensor"),
            P(),
            P(),
            P("dp"),
        ),
        out_specs=(
            P("dp", None, "tensor"),
            P("dp", None, "tensor"),
            P("dp", None, None, "tensor"),
            P(("dp", "tensor"), None, None, None),
        ),
        check_vma=False,
    )
```

```python
import functools
import math

import jax
import jax.numpy as jnp
from jax import lax
from jax.experimental import pallas as pl
from jax.experimental.pallas import tpu as pltpu
from jax.sharding import PartitionSpec as P

HEAD = 128
F32 = jnp.float32
BF16 = jnp.bfloat16
SCALE = HEAD ** (-0.5)
LOG2_SCALE = SCALE * math.log2(math.e)
NT = ((1,), (1,))
NN = ((1,), (0,))
TN = ((0,), (0,))
EVERYONE = ("dp", "tensor")
VMEM_LIMIT = 56 << 20


def dot(a, b, dims):
    return lax.dot_general(a, b, (dims, ((), ())), preferred_element_type=F32)


def attention_kernel(tile_rows, head_block, group, *refs):
    len_ref, query_ref, grad_ref, far_ref, own_key_ref, own_value_ref = refs[:6]
    out_ref, dquery_ref, own_dkey_ref, own_dvalue_ref, far_grad_ref = refs[-9:-4]
    keys, values, dkeys, dvalues = refs[-4:]
    response = pl.program_id(1)
    live_count = len_ref[response]
    row_count = query_ref.shape[1]
    prompt_rows = far_ref.shape[0]
    tall = head_block * tile_rows
    far_rows = pl.ds(0, prompt_rows)
    own_rows = pl.ds(prompt_rows, row_count)

    def hold(rows, key, value):
        keys[rows, :HEAD] = key
        keys[rows, HEAD:] = key
        values[rows, :] = value

    @pl.when(response == 0)
    def _():
        hold(far_rows, far_ref[:, :HEAD], far_ref[:, HEAD:])
        dkeys[:, :prompt_rows] = jnp.zeros((HEAD, prompt_rows), F32)
        dvalues[:, :prompt_rows] = jnp.zeros((HEAD, prompt_rows), F32)

    hold(own_rows, own_key_ref[0], own_value_ref[0])
    dkeys[:, prompt_rows:] = jnp.zeros((HEAD, row_count), F32)
    dvalues[:, prompt_rows:] = jnp.zeros((HEAD, row_count), F32)

    def score(c):
        c["query"] = jnp.concatenate([query_ref[0, c["rows"], s] for s in c["columns"]], 0)
        scaled = c["query"].astype(F32) * LOG2_SCALE
        high = scaled.astype(BF16)
        low = (scaled - high.astype(F32)).astype(BF16)
        c["score"] = dot(jnp.concatenate([high, low], 1), keys[: c["count"]], NT)

    def softmax(c):
        scores, count = c.pop("score"), c["count"]
        row = lax.broadcasted_iota(jnp.int32, (tall, tile_rows), 0) % tile_rows
        column = lax.broadcasted_iota(jnp.int32, (tall, tile_rows), 1)
        corner = jnp.where(column <= row, scores[:, count - tile_rows :], -jnp.inf)
        scores = jnp.concatenate([scores[:, : count - tile_rows], corner], 1)
        exps = jnp.exp2(scores - jnp.max(scores, 1, keepdims=True))
        c["exps"] = exps.astype(BF16)
        place = lax.broadcasted_iota(jnp.int32, (tall, 1), 0) % tile_rows + c["first_row"]
        c["inverse"] = jnp.where(
            place < live_count, 1.0 / jnp.sum(exps, 1, keepdims=True), 0.0
        )

    def attend(c):
        inverse, value = c.pop("inverse"), values[: c["count"]]
        out = (dot(c["exps"], value, NN) * inverse).astype(BF16)
        grad = jnp.concatenate([grad_ref[0, c["rows"], s] for s in c["columns"]], 0)
        c["grad"] = grad = (grad.astype(F32) * inverse).astype(BF16)
        c["delta"] = jnp.sum(grad.astype(F32) * out.astype(F32), 1, keepdims=True)
        for j, s in enumerate(c["columns"]):
            out_ref[0, c["rows"], s] = out[j * tile_rows : (j + 1) * tile_rows]
        c["dprobs"] = dot(grad, value, NT)

    def dscore(c):
        c["dscore"] = c["exps"] * (c.pop("dprobs") - c.pop("delta")).astype(BF16)

    def dquery(c):
        result = (dot(c["dscore"], keys[: c["count"], :HEAD], NN) * SCALE).astype(BF16)
        for j, s in enumerate(c["columns"]):
            dquery_ref[0, c["rows"], s] = result[j * tile_rows : (j + 1) * tile_rows]

    def dkey_dvalue(chains):
        count = chains[0]["count"]
        query, dscores, grad, exps = (
            jnp.concatenate([c.pop(name) for c in chains], 0)
            for name in ("query", "dscore", "grad", "exps")
        )
        dkeys[:, :count] += dot(query, dscores, TN)
        dvalues[:, :count] += dot(grad, exps, TN)

    stages = (score, softmax, attend, dscore, dquery)

    def work(tiles):
        chains = [
            {
                "columns": [pl.ds((h + j) * HEAD, HEAD) for j in range(head_block)],
                "rows": pl.ds(t, tile_rows),
                "first_row": t,
                "count": prompt_rows + t + tile_rows,
            }
            for h in range(0, group, head_block)
            for t in tiles
        ]
        for step in range(len(stages) + len(chains) - 1):
            for i, chain in enumerate(chains):
                if 0 <= step - i < len(stages):
                    stages[step - i](chain)
        for t in tiles:
            dkey_dvalue([c for c in chains if c["first_row"] == t])

    starts = list(range(0, row_count, tile_rows))
    for k in range(len(starts)):
        last = k + 1 == len(starts)
        upper = row_count if last else starts[k + 1]

        @pl.when((live_count > starts[k]) & (last | (live_count <= upper)))
        def _(k=k, last=last, upper=upper):
            work(starts[: k + 1])
            if not last:
                blank = jnp.zeros((row_count - upper, group * HEAD), BF16)
                out_ref[0, upper:, :] = blank
                dquery_ref[0, upper:, :] = blank

    own_dkey_ref[0] = (dkeys[:, prompt_rows:].T * SCALE).astype(BF16)
    own_dvalue_ref[0] = dvalues[:, prompt_rows:].T.astype(BF16)

    @pl.when(response == pl.num_programs(1) - 1)
    def _():
        far_grad_ref[:, :HEAD] = (dkeys[:, :prompt_rows].T * SCALE).astype(BF16)
        far_grad_ref[:, HEAD:] = dvalues[:, :prompt_rows].T.astype(BF16)


def attention_grads(queries, grad_out, own_kv, prefix, resp_len, base, held):
    responses, rows, width = queries.shape
    kv_local = own_kv.shape[2] // (2 * HEAD)
    group = width // HEAD // kv_local
    prompt_rows = prefix.shape[0]
    heads = prefix.shape[1] // (2 * HEAD)
    tile_rows = min(128, rows)
    head_block = math.gcd(group, 4)
    wide = pl.BlockSpec((1, rows, group * HEAD), lambda a, r, *_: (r, 0, a + base))
    own_k = pl.BlockSpec((1, rows, HEAD), lambda a, r, *_: (r, 0, a + base))
    own_v = pl.BlockSpec((1, rows, HEAD), lambda a, r, *_: (r, 0, a + base + kv_local))
    far = pl.BlockSpec((prompt_rows, 2 * HEAD), lambda a, r, *_: (0, a))
    anywhere = pl.BlockSpec(memory_space=pl.ANY)
    own_shape = jax.ShapeDtypeStruct((responses, rows, kv_local * HEAD), BF16)
    pairs = responses * rows * group * heads * (prompt_rows + rows)
    return pl.pallas_call(
        functools.partial(attention_kernel, tile_rows, head_block, group),
        grid_spec=pltpu.PrefetchScalarGridSpec(
            num_scalar_prefetch=1,
            grid=(heads, responses),
            in_specs=[wide, wide, far, own_k, own_v] + [anywhere] * len(held),
            out_specs=[wide, wide, own_k, own_k, far],
            scratch_shapes=[
                pltpu.VMEM((prompt_rows + rows, 2 * HEAD), BF16),
                pltpu.VMEM((prompt_rows + rows, HEAD), BF16),
                pltpu.VMEM((HEAD, prompt_rows + rows), F32),
                pltpu.VMEM((HEAD, prompt_rows + rows), F32),
            ],
        ),
        out_shape=[
            jax.ShapeDtypeStruct(queries.shape, BF16),
            jax.ShapeDtypeStruct(queries.shape, BF16),
            own_shape,
            own_shape,
            jax.ShapeDtypeStruct(prefix.shape, BF16),
        ],
        input_output_aliases={6 + i: i for i in range(len(held))},
        compiler_params=pltpu.CompilerParams(vmem_limit_bytes=VMEM_LIMIT),
        cost_estimate=pl.CostEstimate(
            flops=12 * HEAD * pairs,
            transcendentals=pairs,
            bytes_accessed=8 * responses * rows * group * heads * HEAD,
        ),
        name="attention_grads",
    )(resp_len, queries, grad_out, prefix, own_kv, own_kv, *held)


def outgoing_kernel(tensor_count, kv_local, base, member_ref, slot_ref, pool_ref, out_ref, flat):
    prompts, members = member_ref.shape
    heads = out_ref.shape[2] // (2 * HEAD)
    half = tensor_count * kv_local * HEAD
    for slot in range(pool_ref.shape[1]):
        for part in range(2):
            flat[:, (2 * slot + part) * half : (2 * slot + part + 1) * half] = pool_ref[
                :, slot, part, :
            ]

    def one(i, carry):
        prompt = i // members
        owner = member_ref[prompt, i % members]
        start = slot_ref[prompt] * 2 * half
        for t in range(tensor_count):
            for h in range(heads):
                for part in range(2):
                    source = start + part * half + (t * kv_local + base + h) * HEAD
                    out_ref[owner * tensor_count + t, :, pl.ds((2 * h + part) * HEAD, HEAD)] = flat[
                        :, pl.ds(pl.multiple_of(source, HEAD), HEAD)
                    ]
        return carry

    lax.fori_loop(0, prompts * members, one, 0)


def total_kernel(tensor_count, kv_local, base, member_ref, slot_ref, in_ref, *refs):
    prompts, members = member_ref.shape
    heads = in_ref.shape[2] // (2 * HEAD)
    half = tensor_count * kv_local * HEAD
    flat = refs[-1]
    if len(refs) == 3:
        flat[...] = refs[0][...]

    def one(prompt, carry):
        start = slot_ref[prompt] * 2 * half
        for t in range(tensor_count):
            total = in_ref[member_ref[prompt, 0] * tensor_count + t].astype(F32)
            for m in range(1, members):
                total += in_ref[member_ref[prompt, m] * tensor_count + t].astype(F32)
            total = total.astype(BF16)
            for h in range(heads):
                for part in range(2):
                    target = start + part * half + (t * kv_local + base + h) * HEAD
                    flat[:, pl.ds(pl.multiple_of(target, HEAD), HEAD)] = total[
                        :, (2 * h + part) * HEAD : (2 * h + part + 1) * HEAD
                    ]
        return carry

    lax.fori_loop(0, prompts, one, 0)
    if len(refs) > 1:
        out_ref = refs[-2]
        for slot in range(out_ref.shape[1]):
            for part in range(2):
                out_ref[:, slot, part, :] = flat[
                    :, (2 * slot + part) * half : (2 * slot + part + 1) * half
                ]


def exchange(block, after):
    block, *after = lax.optimization_barrier((block, *after))
    return lax.all_to_all(block, EVERYONE, split_axis=0, concat_axis=0, tiled=True), after


SMEM = pl.BlockSpec(memory_space=pltpu.SMEM)
VMEM = pl.BlockSpec(memory_space=pltpu.VMEM)


def on_device(queries, resp_kv, prefix_pool, grad_out, member_list, prompt_slot, resp_len):
    dp_count = lax.axis_size("dp")
    tensor_count = lax.axis_size("tensor")
    devices = dp_count * tensor_count
    responses, rows = queries.shape[:2]
    kv_width = resp_kv.shape[3]
    kv_local = kv_width // HEAD
    slice_rows, slot_count = prefix_pool.shape[:2]
    shape = (tensor_count, kv_local)
    first = (kv_local + 1) // 2
    chunks = [(0, first)] + ([(first, kv_local - first)] if first < kv_local else [])
    params = pltpu.CompilerParams(vmem_limit_bytes=VMEM_LIMIT)
    pool_width = prefix_pool.size // slice_rows

    def outgoing(base, heads, pool):
        return pl.pallas_call(
            functools.partial(outgoing_kernel, *shape, base),
            in_specs=[SMEM, SMEM, VMEM],
            out_specs=VMEM,
            out_shape=jax.ShapeDtypeStruct((devices, slice_rows, 2 * HEAD * heads), BF16),
            scratch_shapes=[pltpu.VMEM((slice_rows, pool_width), BF16)],
            compiler_params=params,
            name="outgoing_rows",
        )(member_list, prompt_slot, pool)

    def totals(base, block, flat, last):
        held = [] if flat is None else [flat]
        flat_shape = jax.ShapeDtypeStruct((slice_rows, pool_width), BF16)
        return pl.pallas_call(
            functools.partial(total_kernel, *shape, base),
            in_specs=[SMEM, SMEM, VMEM] + [VMEM] * len(held),
            out_specs=VMEM,
            out_shape=jax.ShapeDtypeStruct(prefix_pool.shape, BF16) if last else flat_shape,
            scratch_shapes=[pltpu.VMEM(flat_shape.shape, BF16)] if last else [],
            compiler_params=params,
            name="prefix_totals",
        )(member_list, prompt_slot, block, *held)

    own_kv = resp_kv.reshape(responses, rows, 2 * kv_width)
    prefix, _ = exchange(outgoing(*chunks[0], prefix_pool), ())
    held, flat, arrived = [], None, None
    for k, (base, heads) in enumerate(chunks):
        last = k + 1 == len(chunks)
        if not last:
            ahead = outgoing(*chunks[k + 1], prefix_pool)
            coming, (prefix, own_kv) = exchange(ahead, (prefix, own_kv))
        prefix = prefix.reshape(devices * slice_rows, 2 * HEAD * heads)
        *held, far_grad = attention_grads(
            queries, grad_out, own_kv, prefix, resp_len, base, held
        )
        far_grad = far_grad.reshape(devices, slice_rows, 2 * HEAD * heads)
        if arrived is None:
            arrived, _ = exchange(far_grad, ())
        else:
            following, (arrived,) = exchange(far_grad, (arrived,))
            flat = totals(chunks[k - 1][0], arrived, flat, False)
            arrived = following
        if not last:
            prefix = coming
    attention, grad_queries, own_dkey, own_dvalue = held
    grad_resp_kv = jnp.stack([own_dkey, own_dvalue], axis=2)
    grad_prefix = totals(chunks[-1][0], arrived, flat, True)
    return attention, grad_queries, grad_resp_kv, grad_prefix


def solution(mesh):
    return jax.shard_map(
        on_device,
        mesh=mesh,
        in_specs=(
            P("dp", None, "tensor"),
            P("dp", None, None, "tensor"),
            P(("dp", "tensor"), None, None, None),
            P("dp", None, "tensor"),
            P(),
            P(),
            P("dp"),
        ),
        out_specs=(
            P("dp", None, "tensor"),
            P("dp", None, "tensor"),
            P("dp", None, None, "tensor"),
            P(("dp", "tensor"), None, None, None),
        ),
        check_vma=False,
    )
```

```python
import functools
import math

import jax
import jax.numpy as jnp
from jax import lax
from jax.experimental import pallas as pl
from jax.experimental.pallas import tpu as pltpu
from jax.sharding import PartitionSpec as P

HEAD = 128
F32 = jnp.float32
BF16 = jnp.bfloat16
SCALE = HEAD ** (-0.5)
LOG2_SCALE = SCALE * math.log2(math.e)
NT = ((1,), (1,))
NN = ((1,), (0,))
TN = ((0,), (0,))
EVERYONE = ("dp", "tensor")
VMEM_LIMIT = 56 << 20


def dot(a, b, dims):
    return lax.dot_general(a, b, (dims, ((), ())), preferred_element_type=F32)


def attention_kernel(tile_rows, head_block, group, *refs):
    len_ref, query_ref, grad_ref, far_ref, own_key_ref, own_value_ref = refs[:6]
    out_ref, dquery_ref, own_dkey_ref, own_dvalue_ref, far_grad_ref = refs[-9:-4]
    keys, values, dkeys, dvalues = refs[-4:]
    responses, row_count = query_ref.shape[:2]
    prompt_rows = far_ref.shape[0]
    tall = head_block * tile_rows

    def hold(r, rows, key, value):
        keys[r, rows, :HEAD] = key
        keys[r, rows, HEAD:] = key
        values[r, rows, :] = value

    for r in range(responses):
        hold(r, pl.ds(0, prompt_rows), far_ref[:, :HEAD], far_ref[:, HEAD:])
        hold(r, pl.ds(prompt_rows, row_count), own_key_ref[r], own_value_ref[r])

    def score(c):
        r = c["response"]
        c["query"] = jnp.concatenate([query_ref[r, c["rows"], s] for s in c["columns"]], 0)
        scaled = c["query"].astype(F32) * LOG2_SCALE
        high = scaled.astype(BF16)
        low = (scaled - high.astype(F32)).astype(BF16)
        c["score"] = dot(jnp.concatenate([high, low], 1), keys[r, : c["count"]], NT)

    def softmax(c):
        scores, count = c.pop("score"), c["count"]
        row = lax.broadcasted_iota(jnp.int32, (tall, tile_rows), 0) % tile_rows
        column = lax.broadcasted_iota(jnp.int32, (tall, tile_rows), 1)
        corner = jnp.where(column <= row, scores[:, count - tile_rows :], -jnp.inf)
        scores = jnp.concatenate([scores[:, : count - tile_rows], corner], 1)
        exps = jnp.exp2(scores - jnp.max(scores, 1, keepdims=True))
        c["exps"] = exps.astype(BF16)
        place = lax.broadcasted_iota(jnp.int32, (tall, 1), 0) % tile_rows + c["first_row"]
        c["inverse"] = jnp.where(
            place < len_ref[c["response"]], 1.0 / jnp.sum(exps, 1, keepdims=True), 0.0
        )

    def attend(c):
        r = c["response"]
        inverse, value = c.pop("inverse"), values[r, : c["count"]]
        out = (dot(c["exps"], value, NN) * inverse).astype(BF16)
        grad = jnp.concatenate([grad_ref[r, c["rows"], s] for s in c["columns"]], 0)
        c["grad"] = grad = (grad.astype(F32) * inverse).astype(BF16)
        c["delta"] = jnp.sum(grad.astype(F32) * out.astype(F32), 1, keepdims=True)
        for j, s in enumerate(c["columns"]):
            out_ref[r, c["rows"], s] = out[j * tile_rows : (j + 1) * tile_rows]
        c["dprobs"] = dot(grad, value, NT)

    def dscore(c):
        c["dscore"] = c["exps"] * (c.pop("dprobs") - c.pop("delta")).astype(BF16)

    def dquery(c):
        r = c["response"]
        result = (dot(c["dscore"], keys[r, : c["count"], :HEAD], NN) * SCALE).astype(BF16)
        for j, s in enumerate(c["columns"]):
            dquery_ref[r, c["rows"], s] = result[j * tile_rows : (j + 1) * tile_rows]

    def dkey_dvalue(chains, opening):
        r, count = chains[0]["response"], chains[0]["count"]
        query, dscores, grad, exps = (
            jnp.concatenate([c.pop(name) for c in chains], 0)
            for name in ("query", "dscore", "grad", "exps")
        )
        for ref, block in ((dkeys, dot(query, dscores, TN)), (dvalues, dot(grad, exps, TN))):
            if not opening:
                ref[r, :, :count] += block
                continue
            ref[r, :, :count] = block
            if count < ref.shape[2]:
                ref[r, :, count:] = jnp.zeros((HEAD, ref.shape[2] - count), F32)

    stages = (score, softmax, attend, dscore, dquery)
    blocks = group // head_block

    def work(which, tiles):
        chains = [
            {
                "response": r,
                "columns": [
                    pl.ds((h * head_block + j) * HEAD, HEAD) for j in range(head_block)
                ],
                "rows": pl.ds(t, tile_rows),
                "first_row": t,
                "count": prompt_rows + t + tile_rows,
            }
            for r in which
            for t in reversed(tiles)
            for h in range(blocks)
        ]
        for step in range(len(stages) + len(chains) - 1):
            for i, chain in enumerate(chains):
                if 0 <= step - i < len(stages):
                    stages[step - i](chain)
            ended = step - len(stages) + 2
            if ended > 0 and ended % blocks == 0:
                whole_tile = chains[ended - blocks : ended]
                dkey_dvalue(whole_tile, whole_tile[0]["first_row"] == tiles[-1])

    starts = list(range(0, row_count, tile_rows))
    shortest = len_ref[0]
    for r in range(1, responses):
        shortest = jnp.minimum(shortest, len_ref[r])

    @pl.when(shortest > starts[-1])
    def _():
        work(range(responses), starts)

    @pl.when(shortest <= starts[-1])
    def _():
        def one(r, carry):
            live_count = len_ref[r]
            for k in range(len(starts)):
                last = k + 1 == len(starts)
                upper = row_count if last else starts[k + 1]

                @pl.when((live_count > starts[k]) & (last | (live_count <= upper)))
                def _(k=k, last=last, upper=upper):
                    work([r], starts[: k + 1])
                    if not last:
                        blank = jnp.zeros((row_count - upper, group * HEAD), BF16)
                        out_ref[r, upper:, :] = blank
                        dquery_ref[r, upper:, :] = blank

            return carry

        lax.fori_loop(0, responses, one, 0)

    for r in range(responses):
        own_dkey_ref[r] = (dkeys[r, :, prompt_rows:] * SCALE).astype(BF16).T
        own_dvalue_ref[r] = dvalues[r, :, prompt_rows:].astype(BF16).T
    far = pl.ds(0, prompt_rows)
    far_dkey, far_dvalue = dkeys[0, :, far], dvalues[0, :, far]
    for r in range(1, responses):
        far_dkey += dkeys[r, :, far]
        far_dvalue += dvalues[r, :, far]
    far_grad_ref[:, :HEAD] = (far_dkey * SCALE).astype(BF16).T
    far_grad_ref[:, HEAD:] = far_dvalue.astype(BF16).T


def attention_grads(queries, grad_out, own_kv, prefix, resp_len, base, held):
    responses, rows, width = queries.shape
    kv_local = own_kv.shape[2] // (2 * HEAD)
    group = width // HEAD // kv_local
    prompt_rows = prefix.shape[0]
    heads = prefix.shape[1] // (2 * HEAD)
    tile_rows = min(128, rows)
    head_block = math.gcd(group, 4)
    wide = pl.BlockSpec((responses, rows, group * HEAD), lambda a, *_: (0, 0, a + base))
    own_k = pl.BlockSpec((responses, rows, HEAD), lambda a, *_: (0, 0, a + base))
    own_v = pl.BlockSpec((responses, rows, HEAD), lambda a, *_: (0, 0, a + base + kv_local))
    far = pl.BlockSpec((prompt_rows, 2 * HEAD), lambda a, *_: (0, a))
    anywhere = pl.BlockSpec(memory_space=pl.ANY)
    own_shape = jax.ShapeDtypeStruct((responses, rows, kv_local * HEAD), BF16)
    pairs = responses * rows * group * heads * (prompt_rows + rows)
    return pl.pallas_call(
        functools.partial(attention_kernel, tile_rows, head_block, group),
        grid_spec=pltpu.PrefetchScalarGridSpec(
            num_scalar_prefetch=1,
            grid=(heads,),
            in_specs=[wide, wide, far, own_k, own_v] + [anywhere] * len(held),
            out_specs=[wide, wide, own_k, own_k, far],
            scratch_shapes=[
                pltpu.VMEM((responses, prompt_rows + rows, 2 * HEAD), BF16),
                pltpu.VMEM((responses, prompt_rows + rows, HEAD), BF16),
                pltpu.VMEM((responses, HEAD, prompt_rows + rows), F32),
                pltpu.VMEM((responses, HEAD, prompt_rows + rows), F32),
            ],
        ),
        out_shape=[
            jax.ShapeDtypeStruct(queries.shape, BF16),
            jax.ShapeDtypeStruct(queries.shape, BF16),
            own_shape,
            own_shape,
            jax.ShapeDtypeStruct(prefix.shape, BF16),
        ],
        input_output_aliases={6 + i: i for i in range(len(held))},
        compiler_params=pltpu.CompilerParams(vmem_limit_bytes=VMEM_LIMIT),
        cost_estimate=pl.CostEstimate(
            flops=12 * HEAD * pairs,
            transcendentals=pairs,
            bytes_accessed=8 * responses * rows * group * heads * HEAD,
        ),
        name="attention_grads",
    )(resp_len, queries, grad_out, prefix, own_kv, own_kv, *held)


def outgoing_kernel(tensor_count, kv_local, base, member_ref, slot_ref, pool_ref, out_ref, flat):
    prompts, members = member_ref.shape
    heads = out_ref.shape[2] // (2 * HEAD)
    width = 2 * heads * HEAD
    for slot in range(pool_ref.shape[1]):
        for t in range(tensor_count):
            source = (t * kv_local + base) * HEAD
            for h in range(heads):
                for part in range(2):
                    target = (slot * tensor_count + t) * width + (2 * h + part) * HEAD
                    flat[:, target : target + HEAD] = pool_ref[
                        :, slot, part, source + h * HEAD : source + (h + 1) * HEAD
                    ]

    def one(i, carry):
        prompt = i // members
        owner = member_ref[prompt, i % members]
        for t in range(tensor_count):
            start = pl.multiple_of((slot_ref[prompt] * tensor_count + t) * width, HEAD)
            out_ref[owner * tensor_count + t] = flat[:, pl.ds(start, width)]
        return carry

    lax.fori_loop(0, prompts * members, one, 0)


def total_kernel(tensor_count, kv_local, base, member_ref, slot_ref, in_ref, *refs):
    prompts, members = member_ref.shape
    heads = in_ref.shape[2] // (2 * HEAD)
    out_ref = refs[-1]
    if len(refs) > 1:
        out_ref[...] = refs[0][...]

    def one(prompt, carry):
        for t in range(tensor_count):
            total = in_ref[member_ref[prompt, 0] * tensor_count + t].astype(F32)
            for m in range(1, members):
                total += in_ref[member_ref[prompt, m] * tensor_count + t].astype(F32)
            total = total.astype(BF16)
            for h in range(heads):
                for part in range(2):
                    target = (t * kv_local + base + h) * HEAD
                    out_ref[:, slot_ref[prompt], part, target : target + HEAD] = total[
                        :, (2 * h + part) * HEAD : (2 * h + part + 1) * HEAD
                    ]
        return carry

    lax.fori_loop(0, prompts, one, 0)


def exchange(block, after):
    block, *after = lax.optimization_barrier((block, *after))
    return lax.all_to_all(block, EVERYONE, split_axis=0, concat_axis=0, tiled=True), after


SMEM = pl.BlockSpec(memory_space=pltpu.SMEM)
VMEM = pl.BlockSpec(memory_space=pltpu.VMEM)


def on_device(queries, resp_kv, prefix_pool, grad_out, member_list, prompt_slot, resp_len):
    dp_count = lax.axis_size("dp")
    tensor_count = lax.axis_size("tensor")
    devices = dp_count * tensor_count
    responses, rows = queries.shape[:2]
    kv_width = resp_kv.shape[3]
    kv_local = kv_width // HEAD
    slice_rows, slot_count = prefix_pool.shape[:2]
    shape = (tensor_count, kv_local)
    first = (kv_local + 1) // 2
    chunks = [(0, first)] + ([(first, kv_local - first)] if first < kv_local else [])
    params = pltpu.CompilerParams(vmem_limit_bytes=VMEM_LIMIT)

    def outgoing(base, heads, pool):
        width = slot_count * tensor_count * 2 * HEAD * heads
        return pl.pallas_call(
            functools.partial(outgoing_kernel, *shape, base),
            in_specs=[SMEM, SMEM, VMEM],
            out_specs=VMEM,
            out_shape=jax.ShapeDtypeStruct((devices, slice_rows, 2 * HEAD * heads), BF16),
            scratch_shapes=[pltpu.VMEM((slice_rows, width), BF16)],
            compiler_params=params,
            name="outgoing_rows",
        )(member_list, prompt_slot, pool)

    def totals(base, block, others):
        held = [] if others is None else [others]
        return pl.pallas_call(
            functools.partial(total_kernel, *shape, base),
            in_specs=[SMEM, SMEM, VMEM] + [VMEM] * len(held),
            out_specs=VMEM,
            out_shape=jax.ShapeDtypeStruct(prefix_pool.shape, BF16),
            compiler_params=params,
            name="prefix_totals",
        )(member_list, prompt_slot, block, *held)

    own_kv = resp_kv.reshape(responses, rows, 2 * kv_width)
    prefix, _ = exchange(outgoing(*chunks[0], prefix_pool), ())
    held, summed, arrived = [], None, None
    for k, (base, heads) in enumerate(chunks):
        last = k + 1 == len(chunks)
        if not last:
            ahead = outgoing(*chunks[k + 1], prefix_pool)
            coming, (prefix, own_kv) = exchange(ahead, (prefix, own_kv))
        prefix = prefix.reshape(devices * slice_rows, 2 * HEAD * heads)
        *held, far_grad = attention_grads(
            queries, grad_out, own_kv, prefix, resp_len, base, held
        )
        far_grad = far_grad.reshape(devices, slice_rows, 2 * HEAD * heads)
        if arrived is None:
            arrived, _ = exchange(far_grad, ())
        else:
            following, (arrived,) = exchange(far_grad, (arrived,))
            summed = totals(chunks[k - 1][0], arrived, summed)
            arrived = following
        if not last:
            prefix = coming
    attention, grad_queries, own_dkey, own_dvalue = held
    grad_resp_kv = jnp.stack([own_dkey, own_dvalue], axis=2)
    grad_prefix = totals(chunks[-1][0], arrived, summed)
    return attention, grad_queries, grad_resp_kv, grad_prefix


def solution(mesh):
    return jax.shard_map(
        on_device,
        mesh=mesh,
        in_specs=(
            P("dp", None, "tensor"),
            P("dp", None, None, "tensor"),
            P(("dp", "tensor"), None, None, None),
            P("dp", None, "tensor"),
            P(),
            P(),
            P("dp"),
        ),
        out_specs=(
            P("dp", None, "tensor"),
            P("dp", None, "tensor"),
            P("dp", None, None, "tensor"),
            P(("dp", "tensor"), None, None, None),
        ),
        check_vma=False,
    )
```

```python
import functools
import math

import jax
import jax.numpy as jnp
from jax import lax
from jax.experimental import pallas as pl
from jax.experimental.pallas import tpu as pltpu
from jax.sharding import PartitionSpec as P

HEAD = 128
F32 = jnp.float32
BF16 = jnp.bfloat16
SCALE = HEAD ** (-0.5)
LOG2_SCALE = SCALE * math.log2(math.e)
NT = ((1,), (1,))
NN = ((1,), (0,))
TN = ((0,), (0,))
EVERYONE = ("dp", "tensor")
VMEM_LIMIT = 56 << 20


def dot(a, b, dims):
    return lax.dot_general(a, b, (dims, ((), ())), preferred_element_type=F32)


def attention_kernel(tile_rows, head_block, group, *refs):
    len_ref, query_ref, grad_ref, far_ref, own_key_ref, own_value_ref = refs[:6]
    out_ref, dquery_ref, own_dkey_ref, own_dvalue_ref, far_grad_ref = refs[-9:-4]
    keys, values, dkeys, dvalues = refs[-4:]
    responses, row_count = query_ref.shape[:2]
    prompt_rows = far_ref.shape[0]
    tall = head_block * tile_rows

    def hold(r, rows, key, value):
        keys[r, rows, :HEAD] = key
        keys[r, rows, HEAD:] = key
        values[r, rows, :] = value

    for r in range(responses):
        hold(r, pl.ds(0, prompt_rows), far_ref[:, :HEAD], far_ref[:, HEAD:])
        hold(r, pl.ds(prompt_rows, row_count), own_key_ref[r], own_value_ref[r])

    def score(c):
        r = c["response"]
        c["query"] = jnp.concatenate([query_ref[r, c["rows"], s] for s in c["columns"]], 0)
        scaled = c["query"].astype(F32) * LOG2_SCALE
        high = scaled.astype(BF16)
        low = (scaled - high.astype(F32)).astype(BF16)
        c["score"] = dot(jnp.concatenate([high, low], 1), keys[r, : c["count"]], NT)

    def softmax(c):
        scores, count = c.pop("score"), c["count"]
        row = lax.broadcasted_iota(jnp.int32, (tall, tile_rows), 0) % tile_rows
        column = lax.broadcasted_iota(jnp.int32, (tall, tile_rows), 1)
        corner = jnp.where(column <= row, scores[:, count - tile_rows :], -jnp.inf)
        scores = jnp.concatenate([scores[:, : count - tile_rows], corner], 1)
        exps = jnp.exp2(scores - jnp.max(scores, 1, keepdims=True))
        c["exps"] = exps.astype(BF16)
        place = lax.broadcasted_iota(jnp.int32, (tall, 1), 0) % tile_rows + c["first_row"]
        c["inverse"] = jnp.where(
            place < len_ref[c["response"]], 1.0 / jnp.sum(exps, 1, keepdims=True), 0.0
        )

    def attend(c):
        r = c["response"]
        inverse, value = c.pop("inverse"), values[r, : c["count"]]
        out = (dot(c["exps"], value, NN) * inverse).astype(BF16)
        grad = jnp.concatenate([grad_ref[r, c["rows"], s] for s in c["columns"]], 0)
        c["grad"] = grad = (grad.astype(F32) * inverse).astype(BF16)
        c["delta"] = jnp.sum(grad.astype(F32) * out.astype(F32), 1, keepdims=True)
        for j, s in enumerate(c["columns"]):
            out_ref[r, c["rows"], s] = out[j * tile_rows : (j + 1) * tile_rows]
        c["dprobs"] = dot(grad, value, NT)

    def dscore(c):
        c["dscore"] = c["exps"] * (c.pop("dprobs") - c.pop("delta")).astype(BF16)

    def dquery(c):
        r = c["response"]
        result = (dot(c["dscore"], keys[r, : c["count"], :HEAD], NN) * SCALE).astype(BF16)
        for j, s in enumerate(c["columns"]):
            dquery_ref[r, c["rows"], s] = result[j * tile_rows : (j + 1) * tile_rows]

    def dkey_dvalue(chains, opening):
        r, count = chains[0]["response"], chains[0]["count"]
        query, dscores, grad, exps = (
            jnp.concatenate([c.pop(name) for c in chains], 0)
            for name in ("query", "dscore", "grad", "exps")
        )
        for ref, block in ((dkeys, dot(query, dscores, TN)), (dvalues, dot(grad, exps, TN))):
            if not opening:
                ref[r, :, :count] += block
                continue
            ref[r, :, :count] = block
            if count < ref.shape[2]:
                ref[r, :, count:] = jnp.zeros((HEAD, ref.shape[2] - count), F32)

    stages = (score, softmax, attend, dscore, dquery)
    blocks = group // head_block

    def work(which, tiles):
        chains = [
            {
                "response": r,
                "columns": [
                    pl.ds((h * head_block + j) * HEAD, HEAD) for j in range(head_block)
                ],
                "rows": pl.ds(t, tile_rows),
                "first_row": t,
                "count": prompt_rows + t + tile_rows,
            }
            for t in reversed(tiles)
            for r in which
            for h in range(blocks)
        ]
        for step in range(len(stages) + len(chains) - 1):
            for i, chain in enumerate(chains):
                if 0 <= step - i < len(stages):
                    stages[step - i](chain)
            ended = step - len(stages) + 2
            if ended > 0 and ended % blocks == 0:
                whole_tile = chains[ended - blocks : ended]
                dkey_dvalue(whole_tile, whole_tile[0]["first_row"] == tiles[-1])

    starts = list(range(0, row_count, tile_rows))
    shortest = len_ref[0]
    for r in range(1, responses):
        shortest = jnp.minimum(shortest, len_ref[r])

    @pl.when(shortest > starts[-1])
    def _():
        work(range(responses), starts)

    @pl.when(shortest <= starts[-1])
    def _():
        def one(r, carry):
            live_count = len_ref[r]
            for k in range(len(starts)):
                last = k + 1 == len(starts)
                upper = row_count if last else starts[k + 1]

                @pl.when((live_count > starts[k]) & (last | (live_count <= upper)))
                def _(k=k, last=last, upper=upper):
                    work([r], starts[: k + 1])
                    if not last:
                        blank = jnp.zeros((row_count - upper, group * HEAD), BF16)
                        out_ref[r, upper:, :] = blank
                        dquery_ref[r, upper:, :] = blank

            return carry

        lax.fori_loop(0, responses, one, 0)

    for r in range(responses):
        own_dkey_ref[r] = (dkeys[r, :, prompt_rows:] * SCALE).astype(BF16).T
        own_dvalue_ref[r] = dvalues[r, :, prompt_rows:].astype(BF16).T
    far = pl.ds(0, prompt_rows)
    far_dkey, far_dvalue = dkeys[0, :, far], dvalues[0, :, far]
    for r in range(1, responses):
        far_dkey += dkeys[r, :, far]
        far_dvalue += dvalues[r, :, far]
    far_grad_ref[:, :HEAD] = (far_dkey * SCALE).astype(BF16).T
    far_grad_ref[:, HEAD:] = far_dvalue.astype(BF16).T


def attention_grads(queries, grad_out, own_kv, prefix, resp_len, base, held):
    responses, rows, width = queries.shape
    kv_local = own_kv.shape[2] // (2 * HEAD)
    group = width // HEAD // kv_local
    prompt_rows = prefix.shape[0]
    heads = prefix.shape[1] // (2 * HEAD)
    tile_rows = min(128, rows)
    head_block = math.gcd(group, 4)
    wide = pl.BlockSpec((responses, rows, group * HEAD), lambda a, *_: (0, 0, a + base))
    own_k = pl.BlockSpec((responses, rows, HEAD), lambda a, *_: (0, 0, a + base))
    own_v = pl.BlockSpec((responses, rows, HEAD), lambda a, *_: (0, 0, a + base + kv_local))
    far = pl.BlockSpec((prompt_rows, 2 * HEAD), lambda a, *_: (0, a))
    anywhere = pl.BlockSpec(memory_space=pl.ANY)
    own_shape = jax.ShapeDtypeStruct((responses, rows, kv_local * HEAD), BF16)
    pairs = responses * rows * group * heads * (prompt_rows + rows)
    return pl.pallas_call(
        functools.partial(attention_kernel, tile_rows, head_block, group),
        grid_spec=pltpu.PrefetchScalarGridSpec(
            num_scalar_prefetch=1,
            grid=(heads,),
            in_specs=[wide, wide, far, own_k, own_v] + [anywhere] * len(held),
            out_specs=[wide, wide, own_k, own_k, far],
            scratch_shapes=[
                pltpu.VMEM((responses, prompt_rows + rows, 2 * HEAD), BF16),
                pltpu.VMEM((responses, prompt_rows + rows, HEAD), BF16),
                pltpu.VMEM((responses, HEAD, prompt_rows + rows), F32),
                pltpu.VMEM((responses, HEAD, prompt_rows + rows), F32),
            ],
        ),
        out_shape=[
            jax.ShapeDtypeStruct(queries.shape, BF16),
            jax.ShapeDtypeStruct(queries.shape, BF16),
            own_shape,
            own_shape,
            jax.ShapeDtypeStruct(prefix.shape, BF16),
        ],
        input_output_aliases={6 + i: i for i in range(len(held))},
        compiler_params=pltpu.CompilerParams(vmem_limit_bytes=VMEM_LIMIT),
        cost_estimate=pl.CostEstimate(
            flops=12 * HEAD * pairs,
            transcendentals=pairs,
            bytes_accessed=8 * responses * rows * group * heads * HEAD,
        ),
        name="attention_grads",
    )(resp_len, queries, grad_out, prefix, own_kv, own_kv, *held)


def outgoing_kernel(tensor_count, kv_local, base, member_ref, slot_ref, pool_ref, out_ref, flat):
    prompts, members = member_ref.shape
    heads = out_ref.shape[2] // (2 * HEAD)
    width = 2 * heads * HEAD
    for slot in range(pool_ref.shape[1]):
        for t in range(tensor_count):
            source = (t * kv_local + base) * HEAD
            for h in range(heads):
                place = source + h * HEAD
                pair = pool_ref[:, slot, :, place : place + HEAD].astype(F32)
                for part in range(2):
                    target = (slot * tensor_count + t) * width + (2 * h + part) * HEAD
                    flat[:, target : target + HEAD] = pair[:, part, :].astype(BF16)

    def one(i, carry):
        prompt = i // members
        owner = member_ref[prompt, i % members]
        for t in range(tensor_count):
            start = pl.multiple_of((slot_ref[prompt] * tensor_count + t) * width, HEAD)
            out_ref[owner * tensor_count + t] = flat[:, pl.ds(start, width)]
        return carry

    lax.fori_loop(0, prompts * members, one, 0)


def total_kernel(tensor_count, kv_local, base, member_ref, slot_ref, in_ref, *refs):
    prompts, members = member_ref.shape
    heads = in_ref.shape[2] // (2 * HEAD)
    out_ref = refs[-1]
    if len(refs) > 1:
        out_ref[...] = refs[0][...]

    def one(prompt, carry):
        for t in range(tensor_count):
            total = in_ref[member_ref[prompt, 0] * tensor_count + t].astype(F32)
            for m in range(1, members):
                total += in_ref[member_ref[prompt, m] * tensor_count + t].astype(F32)
            for h in range(heads):
                target = (t * kv_local + base + h) * HEAD
                parts = [total[:, (2 * h + p) * HEAD : (2 * h + p + 1) * HEAD] for p in range(2)]
                out_ref[:, slot_ref[prompt], :, target : target + HEAD] = jnp.stack(
                    parts, axis=1
                ).astype(BF16)
        return carry

    lax.fori_loop(0, prompts, one, 0)


def exchange(block, after):
    block, *after = lax.optimization_barrier((block, *after))
    return lax.all_to_all(block, EVERYONE, split_axis=0, concat_axis=0, tiled=True), after


SMEM = pl.BlockSpec(memory_space=pltpu.SMEM)
VMEM = pl.BlockSpec()


def on_device(queries, resp_kv, prefix_pool, grad_out, member_list, prompt_slot, resp_len):
    dp_count = lax.axis_size("dp")
    tensor_count = lax.axis_size("tensor")
    devices = dp_count * tensor_count
    responses, rows = queries.shape[:2]
    kv_width = resp_kv.shape[3]
    kv_local = kv_width // HEAD
    slice_rows, slot_count = prefix_pool.shape[:2]
    shape = (tensor_count, kv_local)
    first = (kv_local + 1) // 2
    chunks = [(0, first)] + ([(first, kv_local - first)] if first < kv_local else [])
    params = pltpu.CompilerParams(vmem_limit_bytes=VMEM_LIMIT)

    def outgoing(base, heads, pool):
        width = slot_count * tensor_count * 2 * HEAD * heads
        return pl.pallas_call(
            functools.partial(outgoing_kernel, *shape, base),
            in_specs=[SMEM, SMEM, VMEM],
            out_specs=VMEM,
            out_shape=jax.ShapeDtypeStruct((devices, slice_rows, 2 * HEAD * heads), BF16),
            scratch_shapes=[pltpu.VMEM((slice_rows, width), BF16)],
            compiler_params=params,
            name="outgoing_rows",
        )(member_list, prompt_slot, pool)

    def totals(base, block, others):
        held = [] if others is None else [others]
        return pl.pallas_call(
            functools.partial(total_kernel, *shape, base),
            in_specs=[SMEM, SMEM, VMEM] + [VMEM] * len(held),
            out_specs=VMEM,
            out_shape=jax.ShapeDtypeStruct(prefix_pool.shape, BF16),
            compiler_params=params,
            name="prefix_totals",
        )(member_list, prompt_slot, block, *held)

    own_kv = resp_kv.reshape(responses, rows, 2 * kv_width)
    prefix, _ = exchange(outgoing(*chunks[0], prefix_pool), ())
    held, summed, arrived = [], None, None
    for k, (base, heads) in enumerate(chunks):
        last = k + 1 == len(chunks)
        if not last:
            ahead = outgoing(*chunks[k + 1], prefix_pool)
            coming, (prefix, own_kv) = exchange(ahead, (prefix, own_kv))
        prefix = prefix.reshape(devices * slice_rows, 2 * HEAD * heads)
        *held, far_grad = attention_grads(
            queries, grad_out, own_kv, prefix, resp_len, base, held
        )
        far_grad = far_grad.reshape(devices, slice_rows, 2 * HEAD * heads)
        if arrived is None:
            arrived, _ = exchange(far_grad, ())
        else:
            following, (arrived,) = exchange(far_grad, (arrived,))
            summed = totals(chunks[k - 1][0], arrived, summed)
            arrived = following
        if not last:
            prefix = coming
    attention, grad_queries, own_dkey, own_dvalue = held
    grad_resp_kv = jnp.stack([own_dkey, own_dvalue], axis=2)
    grad_prefix = totals(chunks[-1][0], arrived, summed)
    return attention, grad_queries, grad_resp_kv, grad_prefix


def solution(mesh):
    return jax.shard_map(
        on_device,
        mesh=mesh,
        in_specs=(
            P("dp", None, "tensor"),
            P("dp", None, None, "tensor"),
            P(("dp", "tensor"), None, None, None),
            P("dp", None, "tensor"),
            P(),
            P(),
            P("dp"),
        ),
        out_specs=(
            P("dp", None, "tensor"),
            P("dp", None, "tensor"),
            P("dp", None, None, "tensor"),
            P(("dp", "tensor"), None, None, None),
        ),
        check_vma=False,
    )
```
